32 devices in a mesh: kpt: 4 (over y, x), band: 8 (over z, core).
Axes of the slice: x: 2, y: 2, z: 4, core: 2. Of those that a mesh axis runs over, the one named last changes fastest.
Arguments:
- orbitals: bfloat16 [4, 8, 2, 48, 2304], P('kpt', 'band'), may hold values from -6 to 6
- kpoint_coords: int32 [4, 3], replicated, may hold values from 0 to 3, as said below
Outputs:
- exchange: bfloat16 [4, 8, 2, 48, 2304], P('kpt', 'band')
The draws below stay inside these ranges and needn't reach their ends.
Inputs may be any that keep to these rules, and one draw needn't show every extreme that they name: `kpoint_coords`: the 4 rows are distinct points of the 4 x 4 x 4 grid.
All inputs are finite; a program needn't handle non-finite values.
Results may differ from the reference program's by a relative error of at most 0.0075.
The reference program's roundings to bfloat16 on the way (of `density`, `spectrum`, `screened` and `potential`) count: a program that leaves them out, or rounds other values in their place, can miss the bound.
Values may be sent and summed in bfloat16 or wider, within the bound.
A program may use at most 64 MiB of HBM per device.

```python
import math
import jax
import jax.numpy as jnp
from jax import lax

GRID = 48
B_DEV = 1
NK = 4
NB = 8


def draw_kpoint_coords(key, part):
    key = jax.random.fold_in(key, 7)
    order = jax.random.permutation(key, jnp.arange(64, dtype=jnp.int32))
    chosen = order[:NK]
    first = chosen // 16
    second = chosen // 4 % 4
    third = chosen % 4
    return jnp.stack([first, second, third], axis=1).astype(jnp.int32)


def level_of(own_key, extent, shards, low, top_value):
    factor_of = 1.0
    for dim, parts in shards:
        heights = jax.random.uniform(jax.random.fold_in(jax.random.fold_in(own_key, 6), dim), (parts,), jnp.float32, low / len(shards), top_value / len(shards))
        factor_of = factor_of * jnp.repeat(jnp.exp(heights), extent[dim] // parts).reshape((-1,) + (1,) * (len(extent) - 1 - dim))
    return factor_of


def gaussian(own_key, extent, spread, reach, split=(), held_as=jnp.bfloat16):
    entries = spread * jax.random.normal(own_key, extent, jnp.float32)
    if split:
        entries = entries * level_of(own_key, extent, split, -0.22, 0.18)
    return jnp.clip(entries, -reach, reach).astype(held_as)


def setup_inputs(seed: int = 0) -> dict:
    splits = jax.random.split(jax.random.key(seed), 3)
    return {
        "orbitals": gaussian(splits[0], (NK, NB, 2, GRID, GRID * GRID), 1.0, 6.0, ((0, 4), (1, 8))),
        "kpoint_coords": draw_kpoint_coords(jax.random.fold_in(splits[2], 71), 0),
    }


SCREEN = 0.5

def dft_table(points, direction):
    indices = jnp.arange(points, dtype=jnp.int32)
    phases = indices[:, None] * indices[None, :] % points
    angles = phases.astype(jnp.float32) * (2.0 * math.pi / points)
    scaling = 1.0 / math.sqrt(points)
    cosine = jnp.cos(angles) * scaling
    sine_part = direction * jnp.sin(angles) * scaling
    upper_rows = jnp.concatenate([cosine, -sine_part], axis=1)
    lower_rows = jnp.concatenate([sine_part, cosine], axis=1)
    return jnp.concatenate([upper_rows, lower_rows], axis=0).astype(jnp.bfloat16)

def coulomb(coord_first, coord_second, points):
    offset_q = (coord_first - coord_second).astype(jnp.float32) * 0.25
    indices = jnp.arange(points, dtype=jnp.int32)
    frequency = jnp.where(indices < points // 2, indices, indices - points).astype(jnp.float32)
    along_one = (frequency + offset_q[0]) ** 2
    along_two = (frequency + offset_q[1]) ** 2
    along_three = (frequency + offset_q[2]) ** 2
    squared = along_one[:, None, None] + along_two[None, :, None] + along_three[None, None, :]
    cutoff = float((points // 2 - 1) ** 2)
    inside = (squared > 0.0) & (squared <= cutoff)
    values = jnp.where(inside, 4.0 * math.pi / (squared + SCREEN), 0.0)
    return values.reshape(points, points * points).astype(jnp.float32)

def transform(matrix, spectrum, grid_axis):
    pair_count, stacked_rows, grid_cells = spectrum.shape
    points = stacked_rows // 2
    blocked = matrix.astype(jnp.float32).reshape(2, points, 2, points)
    field_cube = spectrum.astype(jnp.float32).reshape(pair_count, 2, points, points, points)
    if grid_axis == 0:
        product = jnp.einsum('aibj,pbjyz->paiyz', blocked, field_cube)
    elif grid_axis == 1:
        product = jnp.einsum('aibj,pbxjz->paxiz', blocked, field_cube)
    else:
        product = jnp.einsum('aibj,pbxyj->paxyi', blocked, field_cube)
    return product.reshape(pair_count, stacked_rows, grid_cells)

def potentials(own_bands, partners, kernel, forward, inverse):
    own_count = own_bands.shape[0]
    partner_count = partners.shape[0]
    points = own_bands.shape[2]
    own_re = own_bands[:, None, 0].astype(jnp.float32)
    own_im = own_bands[:, None, 1].astype(jnp.float32)
    partner_re = partners[None, :, 0].astype(jnp.float32)
    partner_im = partners[None, :, 1].astype(jnp.float32)
    density_re = partner_re * own_re + partner_im * own_im
    density_im = partner_re * own_im - partner_im * own_re
    density = jnp.stack([density_re, density_im], axis=2).astype(jnp.bfloat16)
    spectrum = density.reshape(own_count * partner_count, 2 * points, points * points)
    spectrum = transform(forward, spectrum, 0).astype(jnp.bfloat16)
    spectrum = transform(forward, spectrum, 1).astype(jnp.bfloat16)
    spectrum = transform(forward, spectrum, 2)
    pair_count = spectrum.shape[0]
    screened = (spectrum.reshape(pair_count, 2, points, points * points) * kernel).astype(jnp.bfloat16)
    screened = screened.reshape(pair_count, 2 * points, points * points)
    screened = transform(inverse, screened, 0).astype(jnp.bfloat16)
    screened = transform(inverse, screened, 1).astype(jnp.bfloat16)
    screened = transform(inverse, screened, 2).astype(jnp.bfloat16)
    return screened.reshape(own_count, partner_count, 2, points, points * points)

def to_own(potential, partners):
    pot_re = potential[:, :, 0].astype(jnp.float32)
    pot_im = potential[:, :, 1].astype(jnp.float32)
    partner_re = partners[None, :, 0].astype(jnp.float32)
    partner_im = partners[None, :, 1].astype(jnp.float32)
    real_part = lax.optimization_barrier(jnp.sum(partner_re * pot_re - partner_im * pot_im, axis=1))
    imag_part = lax.optimization_barrier(jnp.sum(partner_re * pot_im + partner_im * pot_re, axis=1))
    return jnp.stack([real_part, imag_part], axis=1)

def to_partner(potential, own_bands):
    pot_re = potential[:, :, 0].astype(jnp.float32)
    pot_im = potential[:, :, 1].astype(jnp.float32)
    own_re = own_bands[:, None, 0].astype(jnp.float32)
    own_im = own_bands[:, None, 1].astype(jnp.float32)
    real_part = lax.optimization_barrier(jnp.sum(own_re * pot_re + own_im * pot_im, axis=0))
    imag_part = lax.optimization_barrier(jnp.sum(own_im * pot_re - own_re * pot_im, axis=0))
    return jnp.stack([real_part, imag_part], axis=1)

def reference(orbitals, kpoint_coords):
    kpoint_count = orbitals.shape[0]
    block_count = orbitals.shape[1] // B_DEV
    points = orbitals.shape[3]
    grouped = orbitals.reshape(kpoint_count, block_count, B_DEV, 2, points, points * points)
    forward = dft_table(points, -1.0)
    inverse = dft_table(points, 1.0)

    def visit(position, accumulated):
        position = jnp.asarray(position).astype(jnp.int32)
        kpoint_at = position // block_count
        block_at = position % block_count
        kpoint_after = (kpoint_at + 1) % kpoint_count
        block_after = (block_at + 1) % block_count
        own_bands = grouped[kpoint_at, block_at]
        next_kpoint = grouped[kpoint_after, block_at]
        next_block = grouped[kpoint_at, block_after]
        kernel_same = coulomb(kpoint_coords[kpoint_at], kpoint_coords[kpoint_at], points)
        kernel_next = coulomb(kpoint_coords[kpoint_at], kpoint_coords[kpoint_after], points)
        potential_own = potentials(own_bands, own_bands, kernel_same, forward, inverse)
        potential_kpoint = potentials(own_bands, next_kpoint, kernel_next, forward, inverse)
        potential_block = potentials(own_bands, next_block, kernel_same, forward, inverse)
        own_part = to_own(potential_own, own_bands) + to_own(potential_kpoint, next_kpoint)
        own_part = own_part + to_own(potential_block, next_block)
        accumulated = accumulated.at[kpoint_at, block_at].add(own_part)
        accumulated = accumulated.at[kpoint_after, block_at].add(to_partner(potential_kpoint, own_bands))
        accumulated = accumulated.at[kpoint_at, block_after].add(to_partner(potential_block, own_bands))
        return accumulated
    initial = jnp.zeros(grouped.shape, jnp.float32)
    accumulated = lax.fori_loop(0, kpoint_count * block_count, visit, initial)
    return (-accumulated).astype(jnp.bfloat16).reshape(orbitals.shape)
```

```python
import functools
import math

import jax
import jax.numpy as jnp
import ml_dtypes
import numpy as np
from jax import lax
from jax.experimental import pallas as pl
from jax.experimental.pallas import tpu as pltpu
from jax.sharding import PartitionSpec as P

SCREEN = 0.5
LANES = 128
GROUP = 4
PITCH_PAD = 8
MESH = pl.DeviceIdType.MESH


def dft_table(points, direction):
    indices = np.arange(points)
    angles = (indices[:, None] * indices[None, :] % points) * (2.0 * math.pi / points)
    scaling = 1.0 / math.sqrt(points)
    cosine = np.cos(angles) * scaling
    sine = direction * np.sin(angles) * scaling
    table = np.block([[cosine, -sine], [sine, cosine]])
    return table.astype(np.float32).astype(ml_dtypes.bfloat16)


def lane_table(points, direction):
    table = dft_table(points, direction).T
    wide = np.zeros((2 * LANES, 2 * LANES), table.dtype)
    for c in range(2):
        for d in range(2):
            block = table[c * points : (c + 1) * points, d * points : (d + 1) * points]
            for p in range(2):
                row, col = c * LANES + p * points, d * LANES + p * points
                wide[row : row + points, col : col + points] = block
    return wide


def dot(a, b):
    return jnp.dot(a, b, preferred_element_type=jnp.float32)


def side(blocks):
    return jnp.concatenate(blocks, axis=1)


def stack(blocks):
    return jnp.concatenate(blocks, axis=0)


def body(
    counts, points, coords, own, wf, wi, zf, zi, out,
    slots, own_wide, part_wide, grid_a, grid_b, total, send_sem, recv_sem,
):
    kpoints, bands = counts
    n = points
    pitch = 2 * n + PITCH_PAD
    bf16, f32 = jnp.bfloat16, jnp.float32
    k, b = lax.axis_index("kpt"), lax.axis_index("band")
    k_step = 1 - 2 * (k % 2)
    b_step = 1 - 2 * (b % 2)
    k_near = (k + k_step + kpoints) % kpoints
    k_far = (k - k_step + kpoints) % kpoints
    b_near = (b + b_step + bands) % bands
    b_far = (b - b_step + bands) % bands
    relay = kpoints == 4
    k_via = (k + 2) % kpoints if relay else k_far

    targets = [(k, b_near), (k_near, b), (k, b_far), (k_via, b)]
    barrier = pltpu.get_barrier_semaphore()
    for target in targets:
        pl.semaphore_signal(barrier, inc=1, device_id=target, device_id_type=MESH)
    pl.semaphore_wait(barrier, len(targets))

    def copy(i, source):
        return pltpu.make_async_remote_copy(
            src_ref=source, dst_ref=slots.at[i], send_sem=send_sem.at[i], recv_sem=recv_sem.at[i],
            device_id=targets[i], device_id_type=MESH,
        )

    copies = [copy(0, own), copy(1, own), copy(2, own), copy(3, slots.at[1] if relay else own)]
    copies[1].start()
    copies[2].start()
    copies[0].start()
    if not relay:
        copies[3].start()

    def widen(target, first, second):
        def chunk(h, carry):
            columns = pl.ds(pl.multiple_of(h * 8 * n, LANES), 8 * n)
            one = first[:, columns]
            two = one if second is first else (None if second is None else second[:, columns])
            blank = jnp.zeros((2 * n, LANES - 2 * n), bf16)
            gap = jnp.zeros((2 * n, n), bf16)
            for j in range(8):
                a = one[:, j * n : (j + 1) * n]
                c = gap if two is None else two[:, j * n : (j + 1) * n]
                target[h * 8 + j] = side([a, c, blank])
            return carry

        lax.fori_loop(0, n // 8, chunk, 0)

    lane = lax.broadcasted_iota(jnp.int32, (1, LANES), 1)
    upper = lane >= n
    z_at = jnp.where(upper, lane - n, lane)
    z_freq = jnp.where(z_at < n // 2, z_at, z_at - n).astype(f32)
    y_at = lax.broadcasted_iota(jnp.int32, (n, LANES), 0)
    y_freq = jnp.where(y_at < n // 2, y_at, y_at - n).astype(f32)
    cutoff = float((n // 2 - 1) ** 2)

    def offsets(first, second):
        def one(p, d):
            return (coords[k, d] - coords[p, d]).astype(f32) * 0.25

        return [jnp.where(upper, one(second, d), one(first, d)) for d in range(3)]

    def batch(first_k, second_k, is_first, between):
        q = offsets(first_k, second_k)
        yz = (y_freq + q[1]) ** 2 + (z_freq + q[2]) ** 2

        def phase_a(g, carry):
            fields = []
            for j in range(GROUP):
                y = g * GROUP + j
                o = own_wide[y].astype(f32)
                p = part_wide[y].astype(f32)
                o_re, o_im, p_re, p_im = o[:n], o[n:], p[:n], p[n:]
                fields.append(stack([p_re * o_re + p_im * o_im, p_re * o_im - p_im * o_re]).astype(bf16))
            r = dot(wf[...], side(fields))
            for j in range(GROUP):
                y = g * GROUP + j
                for c in range(2):
                    grid_a[pl.ds(c * n + y, n, stride=pitch), :] = r[c * n : (c + 1) * n, j * LANES : (j + 1) * LANES]
            return carry

        def planes(ref, g):
            return side(
                [ref[pl.ds(pl.multiple_of((g * GROUP + j) * pitch, 8), 2 * n), :].astype(bf16) for j in range(GROUP)]
            )

        def complex_rows(r):
            rows = []
            for j in range(GROUP):
                part = r[:, j * LANES : (j + 1) * LANES]
                rows.append(side([part[:n], part[n:]]))
            return stack(rows)

        def phase_b(g, carry):
            r = dot(wf[...], planes(grid_a, g)).astype(bf16)
            s = dot(complex_rows(r), zf[...])
            fields = []
            for j in range(GROUP):
                x = g * GROUP + j
                x_freq = jnp.where(x < n // 2, x, x - n).astype(f32)
                squared = (x_freq + q[0]) ** 2 + yz
                inside = (squared > 0.0) & (squared <= cutoff)
                kern = jnp.where(inside, 4.0 * math.pi / (squared + SCREEN), 0.0)
                part = s[j * n : (j + 1) * n]
                fields.append(stack([part[:, :LANES] * kern, part[:, LANES:] * kern]).astype(bf16))
            r = dot(wi[...], side(fields))
            for j in range(GROUP):
                x = g * GROUP + j
                for c in range(2):
                    grid_b[pl.ds(c * n + x, n, stride=pitch), :] = r[c * n : (c + 1) * n, j * LANES : (j + 1) * LANES]
            return carry

        def phase_c(g, carry):
            r = dot(wi[...], planes(grid_b, g)).astype(bf16)
            v = dot(complex_rows(r), zi[...]).astype(bf16).astype(f32)
            for j in range(GROUP):
                y = g * GROUP + j
                p = part_wide[y].astype(f32)
                v_re, v_im = v[j * n : (j + 1) * n, :LANES], v[j * n : (j + 1) * n, LANES:]
                term = stack([p[:n] * v_re - p[n:] * v_im, p[:n] * v_im + p[n:] * v_re])
                total[y] = term if is_first else total[y] + term
            return carry

        lax.fori_loop(0, n // GROUP, phase_a, 0)
        between()
        lax.fori_loop(0, n // GROUP, phase_b, 0)
        lax.fori_loop(0, n // GROUP, phase_c, 0)

    def start_relay():
        copies[1].wait_recv()
        if relay:
            copies[3].start()

    widen(own_wide, own, own)
    copies[0].wait_recv()
    widen(part_wide, own, slots.at[0])
    batch(k, k, True, start_relay)
    copies[2].wait_recv()
    widen(part_wide, slots.at[1], slots.at[2])
    batch(k_near, k, False, lambda: None)
    copies[3].wait_recv()
    widen(part_wide, slots.at[3], None)
    batch(k_far, k, False, lambda: None)

    def finish(h, carry):
        pieces = []
        for j in range(8):
            t = total[h * 8 + j]
            pieces.append(-(t[:, :n] + t[:, n : 2 * n]))
        out[:, pl.ds(pl.multiple_of(h * 8 * n, LANES), 8 * n)] = side(pieces).astype(bf16)
        return carry

    lax.fori_loop(0, n // 8, finish, 0)
    for c in copies:
        c.wait_send()


def on_device(counts, orbitals, kpoint_coords):
    points = orbitals.shape[3]
    cells = orbitals.shape[4]
    n = points
    own = orbitals.reshape(2 * n, cells)
    pitch = 2 * n + PITCH_PAD
    vmem = pl.BlockSpec(memory_space=pltpu.VMEM)
    smem = pl.BlockSpec(memory_space=pltpu.SMEM)
    result = pl.pallas_call(
        functools.partial(body, counts, points),
        out_shape=jax.ShapeDtypeStruct((2 * n, cells), jnp.bfloat16),
        in_specs=[smem] + [vmem] * 5,
        out_specs=vmem,
        scratch_shapes=[
            pltpu.VMEM((4, 2 * n, cells), jnp.bfloat16),
            pltpu.VMEM((n, 2 * n, LANES), jnp.bfloat16),
            pltpu.VMEM((n, 2 * n, LANES), jnp.bfloat16),
            pltpu.VMEM((n * pitch, LANES), jnp.float32),
            pltpu.VMEM((n * pitch, LANES), jnp.float32),
            pltpu.VMEM((n, 2 * n, LANES), jnp.float32),
            pltpu.SemaphoreType.DMA((4,)),
            pltpu.SemaphoreType.DMA((4,)),
        ],
        compiler_params=pltpu.CompilerParams(
            collective_id=0, has_side_effects=True, vmem_limit_bytes=40 * 1024 * 1024
        ),
    )(
        kpoint_coords, own,
        jnp.asarray(dft_table(n, -1.0)), jnp.asarray(dft_table(n, 1.0)),
        jnp.asarray(lane_table(n, -1.0)), jnp.asarray(lane_table(n, 1.0)),
    )
    return result.reshape(orbitals.shape)


def solution(mesh):
    counts = (mesh.shape["kpt"], mesh.shape["band"])
    return jax.shard_map(
        functools.partial(on_device, counts),
        mesh=mesh,
        in_specs=(P("kpt", "band", None, None, None), P()),
        out_specs=P("kpt", "band", None, None, None),
        check_vma=False,
    )
```

```python
import functools
import math

import jax
import jax.numpy as jnp
import ml_dtypes
import numpy as np
from jax import lax
from jax.experimental import pallas as pl
from jax.experimental.pallas import tpu as pltpu
from jax.sharding import PartitionSpec as P

SCREEN = 0.5
LANES = 128
GROUP = 24
SLAB = 8
PITCH_PAD = 8
MESH = pl.DeviceIdType.MESH


def dft_table(points, direction):
    indices = np.arange(points)
    angles = (indices[:, None] * indices[None, :] % points) * (2.0 * math.pi / points)
    scaling = 1.0 / math.sqrt(points)
    cosine = np.cos(angles) * scaling
    sine = direction * np.sin(angles) * scaling
    table = np.block([[cosine, -sine], [sine, cosine]])
    return table.astype(np.float32).astype(ml_dtypes.bfloat16)


def lane_table(points, direction):
    table = dft_table(points, direction).T
    wide = np.zeros((2 * LANES, 2 * LANES), table.dtype)
    for c in range(2):
        for d in range(2):
            block = table[c * points : (c + 1) * points, d * points : (d + 1) * points]
            for p in range(2):
                row, col = c * LANES + p * points, d * LANES + p * points
                wide[row : row + points, col : col + points] = block
    return wide


def dot(a, b):
    return jnp.dot(a, b, preferred_element_type=jnp.float32)


def side(blocks):
    return jnp.concatenate(blocks, axis=1)


def stack(blocks):
    return jnp.concatenate(blocks, axis=0)


def body(
    counts, points, coords_in, own_in, tables_in, out,
    coords, own, tables, local_sem, slots, own_wide, part_wide, grid_a, grid_b, total, send_sem, recv_sem,
):
    kpoints, bands = counts
    n = points
    pitch = 2 * n + PITCH_PAD
    bf16, f32 = jnp.bfloat16, jnp.float32
    k, b = lax.axis_index("kpt"), lax.axis_index("band")
    k_step = 1 - 2 * (k % 2)
    b_step = 1 - 2 * (b % 2)
    k_near = (k + k_step + kpoints) % kpoints
    k_far = (k - k_step + kpoints) % kpoints
    b_near = (b + b_step + bands) % bands
    b_far = (b - b_step + bands) % bands
    relay = kpoints == 4
    k_via = (k + 2) % kpoints if relay else k_far

    targets = [(k, b_near), (k_near, b), (k, b_far), (k_via, b)]
    loads = [
        pltpu.make_async_copy(source, target, local_sem.at[i])
        for i, (source, target) in enumerate(((own_in, own), (tables_in, tables), (coords_in, coords)))
    ]
    for load in loads:
        load.start()
    wide = 2 * LANES
    zf, zi = tables.at[:wide], tables.at[wide : 2 * wide]
    wf = tables.at[2 * wide : 2 * wide + 2 * n, : 2 * n]
    wi = tables.at[2 * wide + 2 * n :, : 2 * n]

    barrier = pltpu.get_barrier_semaphore()
    for target in targets:
        pl.semaphore_signal(barrier, inc=1, device_id=target, device_id_type=MESH)
    pl.semaphore_wait(barrier, len(targets))

    parts = n // SLAB

    def slab(p):
        return pl.ds(pl.multiple_of(p * SLAB * n, LANES), SLAB * n)

    def copy(i, p):
        source = slots.at[1] if relay and i == 3 else own_in
        return pltpu.make_async_remote_copy(
            src_ref=source.at[:, slab(p)], dst_ref=slots.at[i, :, slab(p)],
            send_sem=send_sem.at[i, p], recv_sem=recv_sem.at[i, p],
            device_id=targets[i], device_id_type=MESH,
        )

    def each_part(step):
        def run(p, carry):
            step(p)
            return carry

        lax.fori_loop(0, parts, run, 0)

    def send_near(p):
        copy(0, p).start()

    def send_own(p):
        copy(1, p).start()
        copy(2, p).start()
        if not relay:
            copy(3, p).start()

    each_part(send_near)
    each_part(send_own)
    for load in loads:
        load.wait()

    def pass_on(p):
        copy(1, p).wait_recv()
        if relay:
            copy(3, p).start()

    blank = jnp.zeros((2 * n, LANES - 2 * n), bf16)
    gap = jnp.zeros((2 * n, n), bf16)

    def widen(target, first, second, p):
        one = first[:, slab(p)]
        two = one if second is first else (None if second is None else second[:, slab(p)])
        for j in range(SLAB):
            a = one[:, j * n : (j + 1) * n]
            c = gap if two is None else two[:, j * n : (j + 1) * n]
            target[p * SLAB + j] = side([a, c, blank])

    lane = lax.broadcasted_iota(jnp.int32, (1, LANES), 1)
    upper = lane >= n
    z_at = jnp.where(upper, lane - n, lane)
    z_freq = jnp.where(z_at < n // 2, z_at, z_at - n).astype(f32)
    y_at = lax.broadcasted_iota(jnp.int32, (n, LANES), 0)
    y_freq = jnp.where(y_at < n // 2, y_at, y_at - n).astype(f32)
    cutoff = float((n // 2 - 1) ** 2)

    def offsets(first, second):
        def one(p, d):
            return (coords[k, d] - coords[p, d]).astype(f32) * 0.25

        return [jnp.where(upper, one(second, d), one(first, d)) for d in range(3)]

    def batch(first_k, second_k, is_first, first, second, before, between):
        q = offsets(first_k, second_k)
        yz = (y_freq + q[1]) ** 2 + (z_freq + q[2]) ** 2

        def phase_a(g):
            before(g)
            if is_first:
                widen(own_wide, own, own, g)
            widen(part_wide, first, second, g)
            fields = []
            for j in range(SLAB):
                y = g * SLAB + j
                o = own_wide[y].astype(f32)
                p = part_wide[y].astype(f32)
                o_re, o_im, p_re, p_im = o[:n], o[n:], p[:n], p[n:]
                fields.append(stack([p_re * o_re + p_im * o_im, p_re * o_im - p_im * o_re]).astype(bf16))
            r = dot(wf[...], side(fields))
            for j in range(SLAB):
                y = g * SLAB + j
                for c in range(2):
                    grid_a[pl.ds(c * n + y, n, stride=pitch), :] = r[c * n : (c + 1) * n, j * LANES : (j + 1) * LANES]

        def planes(ref, g):
            return side(
                [ref[pl.ds(pl.multiple_of((g * GROUP + j) * pitch, 8), 2 * n), :].astype(bf16) for j in range(GROUP)]
            )

        def complex_rows(r):
            rows = []
            for j in range(GROUP):
                part = r[:, j * LANES : (j + 1) * LANES]
                rows.append(side([part[:n], part[n:]]))
            return stack(rows)

        def phase_b(g, carry):
            r = dot(wf[...], planes(grid_a, g)).astype(bf16)
            s = dot(complex_rows(r), zf[...])
            fields = []
            for j in range(GROUP):
                x = g * GROUP + j
                x_freq = jnp.where(x < n // 2, x, x - n).astype(f32)
                squared = (x_freq + q[0]) ** 2 + yz
                inside = (squared > 0.0) & (squared <= cutoff)
                kern = jnp.where(inside, 4.0 * math.pi / (squared + SCREEN), 0.0)
                part = s[j * n : (j + 1) * n]
                fields.append(stack([part[:, :LANES] * kern, part[:, LANES:] * kern]).astype(bf16))
            r = dot(wi[...], side(fields))
            for j in range(GROUP):
                x = g * GROUP + j
                for c in range(2):
                    grid_b[pl.ds(c * n + x, n, stride=pitch), :] = r[c * n : (c + 1) * n, j * LANES : (j + 1) * LANES]
            return carry

        def phase_c(g, carry):
            r = dot(wi[...], planes(grid_b, g)).astype(bf16)
            v = dot(complex_rows(r), zi[...]).astype(bf16).astype(f32)
            for j in range(GROUP):
                y = g * GROUP + j
                p = part_wide[y].astype(f32)
                v_re, v_im = v[j * n : (j + 1) * n, :LANES], v[j * n : (j + 1) * n, LANES:]
                term = stack([p[:n] * v_re - p[n:] * v_im, p[:n] * v_im + p[n:] * v_re])
                total[y] = term if is_first else total[y] + term
            return carry

        each_part(phase_a)
        between(0)
        lax.fori_loop(0, n // GROUP, phase_b, 0)
        between(1)
        lax.fori_loop(0, n // GROUP, phase_c, 0)

    def before_second(p):
        @pl.when(p >= 2)
        def _():
            pass_on(p)

        copy(2, p).wait_recv()

    batch(k, k, True, own, slots.at[0], lambda p: copy(0, p).wait_recv(), pass_on)
    batch(k_near, k, False, slots.at[1], slots.at[2], before_second, lambda i: None)
    batch(k_far, k, False, slots.at[3], None, lambda p: copy(3, p).wait_recv(), lambda i: None)

    def finish(h, carry):
        pieces = []
        for j in range(8):
            t = total[h * 8 + j]
            pieces.append(-(t[:, :n] + t[:, n : 2 * n]))
        out[:, pl.ds(pl.multiple_of(h * 8 * n, LANES), 8 * n)] = side(pieces).astype(bf16)
        return carry

    lax.fori_loop(0, n // 8, finish, 0)

    def drain(p):
        for i in range(4):
            copy(i, p).wait_send()

    each_part(drain)


def on_device(counts, orbitals, kpoint_coords):
    points = orbitals.shape[3]
    cells = orbitals.shape[4]
    n = points
    own = orbitals.reshape(2 * n, cells)
    pitch = 2 * n + PITCH_PAD
    tables = np.zeros((4 * LANES + 4 * n, 2 * LANES), ml_dtypes.bfloat16)
    for i, direction in enumerate((-1.0, 1.0)):
        tables[2 * LANES * i : 2 * LANES * (i + 1)] = lane_table(n, direction)
        tables[4 * LANES + 2 * n * i : 4 * LANES + 2 * n * (i + 1), : 2 * n] = dft_table(n, direction)
    result = pl.pallas_call(
        functools.partial(body, counts, points),
        out_shape=jax.ShapeDtypeStruct((2 * n, cells), jnp.bfloat16),
        in_specs=[pl.BlockSpec(memory_space=pl.ANY)] * 3,
        out_specs=pl.BlockSpec(memory_space=pltpu.VMEM),
        scratch_shapes=[
            pltpu.SMEM(kpoint_coords.shape, jnp.int32),
            pltpu.VMEM((2 * n, cells), jnp.bfloat16),
            pltpu.VMEM(tables.shape, jnp.bfloat16),
            pltpu.SemaphoreType.DMA((3,)),
            pltpu.VMEM((4, 2 * n, cells), jnp.bfloat16),
            pltpu.VMEM((n, 2 * n, LANES), jnp.bfloat16),
            pltpu.VMEM((n, 2 * n, LANES), jnp.bfloat16),
            pltpu.VMEM((n * pitch, LANES), jnp.float32),
            pltpu.VMEM((n * pitch, LANES), jnp.float32),
            pltpu.VMEM((n, 2 * n, LANES), jnp.float32),
            pltpu.SemaphoreType.DMA((4, n // SLAB)),
            pltpu.SemaphoreType.DMA((4, n // SLAB)),
        ],
        compiler_params=pltpu.CompilerParams(
            collective_id=0, has_side_effects=True, vmem_limit_bytes=60 * 1024 * 1024
        ),
    )(
        kpoint_coords, own, jnp.asarray(tables),
    )
    return result.reshape(orbitals.shape)


def solution(mesh):
    counts = (mesh.shape["kpt"], mesh.shape["band"])
    return jax.shard_map(
        functools.partial(on_device, counts),
        mesh=mesh,
        in_specs=(P("kpt", "band", None, None, None), P()),
        out_specs=P("kpt", "band", None, None, None),
        check_vma=False,
    )
```
